512 devices in a mesh: row: 16 (over y_lo, x, core), col: 32 (over z, y_hi).
Axes of the slice: x: 4, y: 8 (y_hi: 4, y_lo: 2; y = y_hi * 2 + y_lo), z: 8, core: 2. Of those that a mesh axis runs over, the one named last changes fastest.
Arguments:
- panel: bfloat16 [16, 32, 128, 512], P('row', 'col'), may hold values from -6 to 6
- blocks: bfloat16 [16, 32, 128, 128, 128], P('row', 'col'), may hold values from -0.0625 to 0.0625
- block_rows: int32 [16, 32, 128], P('row', 'col'), may hold values from 0 to 31
- block_cols: int32 [16, 32, 128], P('row', 'col'), may hold values from 0 to 15
- block_count: int32 [16, 32], P('row', 'col'), may hold values from 16 to 128, as said below
- pre_act: bfloat16 [32, 16, 128, 512], P('col', 'row'), may hold values from -6 to 6
Outputs:
- grad_input: bfloat16 [32, 16, 128, 512], P('col', 'row')
The draws below stay inside these ranges and needn't reach their ends.
Inputs may be any that keep to these rules, and one draw needn't show every extreme that they name: `block_count`: some device has exactly 128 live slots and some exactly 16; counts are 128 divided by 1, 2, 4 or 8.
All inputs are finite; a program needn't handle non-finite values.
Results may differ from the reference program's by a relative error of at most 0.015.
Values may be sent and summed in bfloat16 or wider, within the bound.
No kernel may reach another device: no remote copies, remote signals or barrier semaphores. Data moves between devices by JAX's collectives and lax.ppermute only.
A program may use at most 128 MiB of HBM per device.

```python
import jax
import jax.numpy as jnp
from jax import lax

BS = 128
F = 512
NB_DEV = 128
BROWS = 32
BC_DEV = 16
N_ROW = 16
N_COL = 32


def draw_block_count(key, part):
    key = jax.random.fold_in(key, 7)
    first, second = jax.random.split(key)
    tiers = jax.random.randint(first, (N_ROW * N_COL,), 0, 4)
    counts = NB_DEV // 2 ** tiers
    chosen = jax.random.randint(second, (), 0, N_ROW * N_COL)
    counts = counts.at[chosen].set(NB_DEV)
    counts = counts.at[(chosen + 1) % (N_ROW * N_COL)].set(NB_DEV // 8)
    return counts.reshape(N_ROW, N_COL).astype(jnp.int32)


def place_ends(values, stream_key, low, top_value):
    shape = values.shape
    index_at = [jax.random.randint(jax.random.fold_in(stream_key, axis), (), 0, shape[axis]) for axis in range(len(shape))]
    values = values.at[tuple(index_at)].set(low)
    longest = shape.index(max(shape))
    index_at[longest] = (index_at[longest] + 1) % shape[longest]
    return values.at[tuple(index_at)].set(top_value)


def levels(own_key, shape, cuts, smallest, top_value):
    loudness, own = 1.0, jax.random.fold_in(own_key, 6)
    for dim, shards_of in cuts:
        heights = jnp.exp(jax.random.uniform(jax.random.fold_in(own, dim), (shards_of,), jnp.float32, smallest / len(cuts), top_value / len(cuts)))
        loudness = loudness * jnp.repeat(heights, shape[dim] // shards_of).reshape([-1 if axis == dim else 1 for axis in range(len(shape))])
    return loudness


def scatter_about(key, shape, width, most, shards=(), held_as=jnp.bfloat16):
    values = jax.random.normal(key, shape, jnp.float32) * width
    if len(shards) > 0:
        values = levels(key, shape, shards, -0.22, 0.18) * values
    return jnp.clip(values, min=-most, max=most).astype(held_as)


def setup_inputs(seed: int = 0) -> dict:
    keys = jax.random.split(jax.random.key(seed), 7)
    return {
        "panel": scatter_about(keys[0], (N_ROW, BROWS, BS, F), 1.0, 6.0, ((0, 16), (1, 32))),
        "blocks": scatter_about(keys[1], (N_ROW, N_COL, NB_DEV, BS, BS), (BS * NB_DEV // 2) ** -0.5, 0.0625, ((0, 16), (1, 32))),
        "block_rows": place_ends(jax.random.randint(keys[2], (N_ROW, N_COL, NB_DEV), 0, BROWS), jax.random.fold_in(keys[2], 1), 0, BROWS - 1).astype(jnp.int32),
        "block_cols": place_ends(jax.random.randint(keys[3], (N_ROW, N_COL, NB_DEV), 0, BC_DEV), jax.random.fold_in(keys[3], 1), 0, BC_DEV - 1).astype(jnp.int32),
        "block_count": draw_block_count(jax.random.fold_in(keys[6], 71), 0),
        "pre_act": scatter_about(keys[5], (N_COL, BC_DEV, BS, F), 1.0, 6.0, ((0, 32), (1, 16))),
    }


def reference(panel, blocks, block_rows, block_cols, block_count, pre_act):
    nrows = blocks.shape[0]
    ncols = blocks.shape[1]
    slots = blocks.shape[2]

    def device_step(total, index):
        rgrp = index // ncols
        cgrp = index % ncols
        values = blocks[rgrp, cgrp].astype(jnp.float32)
        picked = panel[rgrp][block_rows[rgrp, cgrp]].astype(jnp.float32)
        prod = jnp.einsum('bij,bif->bjf', values, picked, precision=lax.Precision.HIGHEST)
        live = lax.iota(jnp.int32, slots) < block_count[rgrp, cgrp]
        prod = jnp.where(live[:, None, None], prod, jnp.float32(0.0))
        part = jnp.zeros((BC_DEV, BS, F), jnp.float32).at[block_cols[rgrp, cgrp]].add(prod)
        return total.at[cgrp].add(part), None

    start = jnp.zeros((N_COL, BC_DEV, BS, F), jnp.float32)
    total, _ = lax.scan(device_step, start, lax.iota(jnp.int32, nrows * ncols))
    return jnp.where(pre_act > 0, total, jnp.float32(0.0)).astype(jnp.bfloat16)
```

```python
import functools
import itertools

import jax
import jax.numpy as jnp
from jax import lax
from jax.experimental import pallas as pl
from jax.experimental.pallas import tpu as pltpu
from jax.sharding import PartitionSpec as P

YL, X, CORE, Z, YH = 2, 4, 2, 8, 4
AXES = ("row", "col")
GROUP = 16
PARTS = 2


def place(yl, x, core, z, yh):
    row = ((yl % YL) * X + x % X) * CORE + core % CORE
    return row * (Z * YH) + (z % Z) * YH + yh % YH


def moves(step):
    spots = itertools.product(range(YL), range(X), range(CORE), range(Z), range(YH))
    return [(place(*spot), place(*step(*spot))) for spot in spots]


def along_y(by):
    return lambda yl, x, core, z, yh: (yl, x, core, z, yh + by)


def along_z(by):
    return lambda yl, x, core, z, yh: (yl, x, core, z + by, yh)


def other_core(yl, x, core, z, yh):
    return yl, x, core + 1, z, yh


def send(value, step):
    return lax.ppermute(value, AXES, moves(step))


def spmm_kernel(first, meta, blocks, *refs):
    pieces = refs[:-7]
    keep, away, vals, pan, acc, piece_sem, block_sem = refs[-7:]
    sizes = [piece.shape[0] for piece in pieces]
    starts = [sum(sizes[:k]) for k in range(len(sizes))]
    slots = blocks.shape[0]
    count = meta[2 * slots]
    core = meta[2 * slots + 1]
    groups = count // GROUP

    def block_copy(g):
        part = pl.ds(g * GROUP, GROUP)
        return pltpu.make_async_copy(blocks.at[part], vals.at[part], block_sem.at[g])

    def piece_copy(k):
        part = pieces[k].at[:, :, pl.ds(first, pan.shape[2])]
        return pltpu.make_async_copy(part, pan.at[pl.ds(starts[k], sizes[k])], piece_sem.at[k])

    block_copy(0).start()
    for k in range(len(pieces)):
        piece_copy(k).start()

    @pl.loop(1, groups)
    def _(g):
        block_copy(g).start()

    acc[...] = jnp.zeros_like(acc)
    for k in range(len(pieces)):
        piece_copy(k).wait()

    @pl.loop(0, groups)
    def _(g):
        block_copy(g).wait()
        for s in range(GROUP):
            slot = g * GROUP + s
            prod = lax.dot_general(
                vals[slot], pan[meta[slot]], (((0,), (0,)), ((), ())), preferred_element_type=jnp.float32
            )
            col = meta[slots + slot]
            acc[col] = acc[col] + prod

    for k in range(keep.shape[0]):
        keep[k] = acc[CORE * k + core]
        away[k] = acc[CORE * k + 1 - core].astype(away.dtype)


def spmm(meta, values, pieces, first, width):
    slots, bs = values.shape[0], values.shape[1]
    blocks_out = YL * X
    anywhere = pl.BlockSpec(memory_space=pl.ANY)
    return pl.pallas_call(
        functools.partial(spmm_kernel, first),
        out_shape=(
            jax.ShapeDtypeStruct((blocks_out, bs, width), jnp.float32),
            jax.ShapeDtypeStruct((blocks_out, bs, width), jnp.bfloat16),
        ),
        in_specs=[pl.BlockSpec(memory_space=pltpu.SMEM), pl.BlockSpec(memory_space=pltpu.HBM)]
        + [anywhere] * len(pieces),
        out_specs=[pl.BlockSpec(memory_space=pltpu.VMEM)] * 2,
        scratch_shapes=[
            pltpu.VMEM(values.shape, jnp.bfloat16),
            pltpu.VMEM((Z * YH, bs, width), jnp.bfloat16),
            pltpu.VMEM((blocks_out * CORE, bs, width), jnp.float32),
            pltpu.SemaphoreType.DMA((len(pieces),)),
            pltpu.SemaphoreType.DMA((slots // GROUP,)),
        ],
        compiler_params=pltpu.CompilerParams(vmem_limit_bytes=32 * 2**20),
        cost_estimate=pl.CostEstimate(
            flops=2 * slots * bs * bs * width, bytes_accessed=8 * 2**20, transcendentals=0
        ),
    )(meta, values, *pieces)


def combine_kernel(keep, came, out):
    out[...] = (keep[...] + came[...].astype(jnp.float32)).astype(out.dtype)


def combine(keep, came):
    whole = pl.BlockSpec(memory_space=pltpu.VMEM)
    return pl.pallas_call(
        combine_kernel,
        out_shape=jax.ShapeDtypeStruct(keep.shape, jnp.bfloat16),
        in_specs=[whole, whole],
        out_specs=whole,
        compiler_params=pltpu.CompilerParams(vmem_limit_bytes=16 * 2**20),
        cost_estimate=pl.CostEstimate(flops=keep.size, bytes_accessed=8 * keep.size, transcendentals=0),
    )(keep, came)


def finish_kernel(pre, *refs):
    out = refs[-1]
    width = pre.shape[1] // PARTS
    for part in range(PARTS):
        terms = refs[part]
        total = terms[0].astype(jnp.float32)
        for k in range(1, YL * X):
            total = total + terms[k].astype(jnp.float32)
        cols = slice(part * width, (part + 1) * width)
        gate = pre[:, cols].astype(jnp.float32) > 0
        out[:, cols] = jnp.where(gate, total, 0.0).astype(out.dtype)


def finish(pre, terms):
    whole = pl.BlockSpec(memory_space=pltpu.VMEM)
    return pl.pallas_call(
        finish_kernel,
        out_shape=jax.ShapeDtypeStruct(pre.shape, jnp.bfloat16),
        in_specs=[whole] * (1 + len(terms)),
        out_specs=whole,
        compiler_params=pltpu.CompilerParams(vmem_limit_bytes=16 * 2**20),
        cost_estimate=pl.CostEstimate(flops=9 * pre.size, bytes_accessed=20 * pre.size, transcendentals=0),
    )(pre, *terms)


def gather_column(part):
    return [part, send(part, along_y(1)), send(part, along_y(2)), send(part, along_y(-1))]


def gather_rings(mine):
    low, high = [mine], [mine]
    for _ in range(Z // 2 - 1):
        low.append(send(low[-1], along_z(1)))
        high.append(send(high[-1], along_z(-1)))
    cut = YH // 2
    middle = [send(low[-1][:cut], along_z(1)), send(high[-1][cut:], along_z(-1))]
    return low + middle + high[:0:-1]


def reduce_part(keep, away):
    both = combine(keep, send(away, other_core))
    groups = [[CORE * k + core for k in range(YL * X)] for core in range(CORE)]
    return lax.all_to_all(both, "row", 0, 0, axis_index_groups=groups, tiled=True)


def shards(panel, blocks, block_rows, block_cols, block_count, pre_act):
    values = blocks[0, 0]
    col = lax.axis_index("col")
    core = (lax.axis_index("row") & 1).astype(jnp.int32)
    z, yh = col >> 2, col & (YH - 1)
    rows = block_rows[0, 0]
    near = ((z - (rows >> 2)) & (Z - 1)) * YH + ((yh - rows) & (YH - 1))
    meta = jnp.concatenate([near, block_cols[0, 0], block_count[0], core[None]])

    width = panel.shape[3] // PARTS
    column = gather_column(panel[0, 0])
    pieces = gather_rings(jnp.stack(column))
    parts = [spmm(meta, values, pieces, p * width, width) for p in range(PARTS)]
    terms = [reduce_part(*part) for part in parts]
    return finish(pre_act[0, 0], terms)[None, None]


def solution(mesh):
    placed = (
        P("row", "col", None, None),
        P("row", "col", None, None, None),
        P("row", "col", None),
        P("row", "col", None),
        P("row", "col"),
        P("col", "row", None, None),
    )
    return jax.shard_map(
        shards, mesh=mesh, in_specs=placed, out_specs=P("col", "row", None, None), check_vma=False
    )
```

```python
import functools
import itertools

import jax
import jax.numpy as jnp
from jax import lax
from jax.experimental import pallas as pl
from jax.experimental.pallas import tpu as pltpu
from jax.sharding import PartitionSpec as P

YL, X, CORE, Z, YH = 2, 4, 2, 8, 4
AXES = ("row", "col")
GROUP = 16
PARTS = 1


def place(yl, x, core, z, yh):
    row = ((yl % YL) * X + x % X) * CORE + core % CORE
    return row * (Z * YH) + (z % Z) * YH + yh % YH


def moves(step):
    spots = itertools.product(range(YL), range(X), range(CORE), range(Z), range(YH))
    return [(place(*spot), place(*step(*spot))) for spot in spots]


def along_y(by):
    return lambda yl, x, core, z, yh: (yl, x, core, z, yh + by)


def along_z(by):
    return lambda yl, x, core, z, yh: (yl, x, core, z + by, yh)


def other_core(yl, x, core, z, yh):
    return yl, x, core + 1, z, yh


def send(value, step):
    return lax.ppermute(value, AXES, moves(step))


def spmm_kernel(first, meta, blocks, *refs):
    pieces = refs[:-7]
    keep, away, vals, pan, acc, piece_sem, block_sem = refs[-7:]
    sizes = [piece.shape[0] for piece in pieces]
    starts = [sum(sizes[:k]) for k in range(len(sizes))]
    slots = blocks.shape[0]
    count = meta[2 * slots]
    core = meta[2 * slots + 1]
    groups = count // GROUP

    def block_copy(g):
        part = pl.ds(g * GROUP, GROUP)
        return pltpu.make_async_copy(blocks.at[part], vals.at[part], block_sem.at[g])

    def piece_copy(k):
        part = pieces[k].at[:, :, pl.ds(first, pan.shape[2])]
        return pltpu.make_async_copy(part, pan.at[pl.ds(starts[k], sizes[k])], piece_sem.at[k])

    block_copy(0).start()
    for k in range(len(pieces)):
        piece_copy(k).start()

    @pl.loop(1, groups)
    def _(g):
        block_copy(g).start()

    acc[...] = jnp.zeros_like(acc)
    for k in range(len(pieces)):
        piece_copy(k).wait()

    @pl.loop(0, groups)
    def _(g):
        block_copy(g).wait()
        for s in range(GROUP):
            slot = g * GROUP + s
            prod = lax.dot_general(
                vals[slot], pan[meta[slot]], (((0,), (0,)), ((), ())), preferred_element_type=jnp.float32
            )
            col = meta[slots + slot]
            acc[col] = acc[col] + prod

    for k in range(keep.shape[0]):
        keep[k] = acc[CORE * k + core]
        away[k] = acc[CORE * k + 1 - core].astype(away.dtype)


def spmm(meta, values, pieces, first, width):
    slots, bs = values.shape[0], values.shape[1]
    blocks_out = YL * X
    anywhere = pl.BlockSpec(memory_space=pl.ANY)
    return pl.pallas_call(
        functools.partial(spmm_kernel, first),
        out_shape=(
            jax.ShapeDtypeStruct((blocks_out, bs, width), jnp.float32),
            jax.ShapeDtypeStruct((blocks_out, bs, width), jnp.bfloat16),
        ),
        in_specs=[pl.BlockSpec(memory_space=pltpu.SMEM), pl.BlockSpec(memory_space=pltpu.HBM)]
        + [anywhere] * len(pieces),
        out_specs=[pl.BlockSpec(memory_space=pltpu.VMEM)] * 2,
        scratch_shapes=[
            pltpu.VMEM(values.shape, jnp.bfloat16),
            pltpu.VMEM((Z * YH, bs, width), jnp.bfloat16),
            pltpu.VMEM((blocks_out * CORE, bs, width), jnp.float32),
            pltpu.SemaphoreType.DMA((len(pieces),)),
            pltpu.SemaphoreType.DMA((slots // GROUP,)),
        ],
        compiler_params=pltpu.CompilerParams(vmem_limit_bytes=32 * 2**20),
        cost_estimate=pl.CostEstimate(
            flops=2 * slots * bs * bs * width, bytes_accessed=8 * 2**20, transcendentals=0
        ),
    )(meta, values, *pieces)


def combine_kernel(keep, came, out):
    out[...] = (keep[...] + came[...].astype(jnp.float32)).astype(out.dtype)


def combine(keep, came):
    whole = pl.BlockSpec(memory_space=pltpu.VMEM)
    return pl.pallas_call(
        combine_kernel,
        out_shape=jax.ShapeDtypeStruct(keep.shape, jnp.bfloat16),
        in_specs=[whole, whole],
        out_specs=whole,
        compiler_params=pltpu.CompilerParams(vmem_limit_bytes=16 * 2**20),
        cost_estimate=pl.CostEstimate(flops=keep.size, bytes_accessed=8 * keep.size, transcendentals=0),
    )(keep, came)


def finish_kernel(pre, *refs):
    out = refs[-1]
    width = pre.shape[1] // PARTS
    for part in range(PARTS):
        terms = refs[part]
        total = terms[0].astype(jnp.float32)
        for k in range(1, YL * X):
            total = total + terms[k].astype(jnp.float32)
        cols = slice(part * width, (part + 1) * width)
        gate = pre[:, cols].astype(jnp.float32) > 0
        out[:, cols] = jnp.where(gate, total, 0.0).astype(out.dtype)


def finish(pre, terms):
    whole = pl.BlockSpec(memory_space=pltpu.VMEM)
    return pl.pallas_call(
        finish_kernel,
        out_shape=jax.ShapeDtypeStruct(pre.shape, jnp.bfloat16),
        in_specs=[whole] * (1 + len(terms)),
        out_specs=whole,
        compiler_params=pltpu.CompilerParams(vmem_limit_bytes=16 * 2**20),
        cost_estimate=pl.CostEstimate(flops=9 * pre.size, bytes_accessed=20 * pre.size, transcendentals=0),
    )(pre, *terms)


def gather_column(part):
    return [part, send(part, along_y(1)), send(part, along_y(2)), send(part, along_y(-1))]


def gather_rings(mine):
    low, high = [mine], [mine]
    for _ in range(Z // 2 - 1):
        low.append(send(low[-1], along_z(1)))
        high.append(send(high[-1], along_z(-1)))
    cut = YH // 2
    middle = [send(low[-1][:cut], along_z(1)), send(high[-1][cut:], along_z(-1))]
    return low + middle + high[:0:-1]


def reduce_part(keep, away):
    both = combine(keep, send(away, other_core))
    groups = [[CORE * k + core for k in range(YL * X)] for core in range(CORE)]
    return lax.all_to_all(both, "row", 0, 0, axis_index_groups=groups, tiled=True)


def shards(panel, blocks, block_rows, block_cols, block_count, pre_act):
    values = blocks[0, 0]
    col = lax.axis_index("col")
    core = (lax.axis_index("row") & 1).astype(jnp.int32)
    z, yh = col >> 2, col & (YH - 1)
    rows = block_rows[0, 0]
    near = ((z - (rows >> 2)) & (Z - 1)) * YH + ((yh - rows) & (YH - 1))
    meta = jnp.concatenate([near, block_cols[0, 0], block_count[0], core[None]])

    width = panel.shape[3] // PARTS
    column = gather_column(panel[0, 0])
    pieces = gather_rings(jnp.stack(column))
    parts = [spmm(meta, values, pieces, p * width, width) for p in range(PARTS)]
    terms = [reduce_part(*part) for part in parts]
    return finish(pre_act[0, 0], terms)[None, None]


def solution(mesh):
    placed = (
        P("row", "col", None, None),
        P("row", "col", None, None, None),
        P("row", "col", None),
        P("row", "col", None),
        P("row", "col"),
        P("col", "row", None, None),
    )
    return jax.shard_map(
        shards, mesh=mesh, in_specs=placed, out_specs=P("col", "row", None, None), check_vma=False
    )
```

```python
import functools
import itertools

import jax
import jax.numpy as jnp
from jax import lax
from jax.experimental import pallas as pl
from jax.experimental.pallas import tpu as pltpu
from jax.sharding import PartitionSpec as P

YL, X, CORE, Z, YH = 2, 4, 2, 8, 4
AXES = ("row", "col")
GROUP = 16
PARTS = 1


def place(yl, x, core, z, yh):
    row = ((yl % YL) * X + x % X) * CORE + core % CORE
    return row * (Z * YH) + (z % Z) * YH + yh % YH


def moves(step):
    spots = itertools.product(range(YL), range(X), range(CORE), range(Z), range(YH))
    return [(place(*spot), place(*step(*spot))) for spot in spots]


def along_y(by):
    return lambda yl, x, core, z, yh: (yl, x, core, z, yh + by)


def along_z(by):
    return lambda yl, x, core, z, yh: (yl, x, core, z + by, yh)


def other_core(yl, x, core, z, yh):
    return yl, x, core + 1, z, yh


def send(value, step):
    return lax.ppermute(value, AXES, moves(step))


def fetch_kernel(meta, blocks, vals, sem):
    groups = meta[2 * blocks.shape[0]] // GROUP

    def block_copy(g):
        part = pl.ds(g * GROUP, GROUP)
        return pltpu.make_async_copy(blocks.at[part], vals.at[part], sem.at[g])

    @pl.loop(0, groups)
    def _(g):
        block_copy(g).start()

    @pl.loop(0, groups)
    def _(g):
        block_copy(g).wait()


def fetch(meta, values):
    return pl.pallas_call(
        fetch_kernel,
        out_shape=jax.ShapeDtypeStruct(values.shape, values.dtype),
        in_specs=[pl.BlockSpec(memory_space=pltpu.SMEM), pl.BlockSpec(memory_space=pltpu.HBM)],
        out_specs=pl.BlockSpec(memory_space=pltpu.VMEM),
        scratch_shapes=[pltpu.SemaphoreType.DMA((values.shape[0] // GROUP,))],
        compiler_params=pltpu.CompilerParams(vmem_limit_bytes=16 * 2**20),
        cost_estimate=pl.CostEstimate(flops=0, bytes_accessed=2 * values.size, transcendentals=0),
    )(meta, values)


def spmm_kernel(first, meta, vals, *refs):
    pieces = refs[:-5]
    keep, away, pan, acc, piece_sem = refs[-5:]
    sizes = [piece.shape[0] for piece in pieces]
    starts = [sum(sizes[:k]) for k in range(len(sizes))]
    slots = vals.shape[0]
    count = meta[2 * slots]
    core = meta[2 * slots + 1]
    def piece_copy(k):
        part = pieces[k].at[:, :, pl.ds(first, pan.shape[2])]
        return pltpu.make_async_copy(part, pan.at[pl.ds(starts[k], sizes[k])], piece_sem.at[k])

    for k in range(len(pieces)):
        piece_copy(k).start()

    acc[...] = jnp.zeros_like(acc)
    for k in range(len(pieces)):
        piece_copy(k).wait()

    @pl.loop(0, count // GROUP)
    def _(g):
        for s in range(GROUP):
            slot = g * GROUP + s
            prod = lax.dot_general(
                vals[slot], pan[meta[slot]], (((0,), (0,)), ((), ())), preferred_element_type=jnp.float32
            )
            col = meta[slots + slot]
            acc[col] = acc[col] + prod

    for k in range(keep.shape[0]):
        keep[k] = acc[CORE * k + core]
        away[k] = acc[CORE * k + 1 - core].astype(away.dtype)


def spmm(meta, values, pieces, first, width):
    slots, bs = values.shape[0], values.shape[1]
    blocks_out = YL * X
    anywhere = pl.BlockSpec(memory_space=pl.ANY)
    return pl.pallas_call(
        functools.partial(spmm_kernel, first),
        out_shape=(
            jax.ShapeDtypeStruct((blocks_out, bs, width), jnp.float32),
            jax.ShapeDtypeStruct((blocks_out, bs, width), jnp.bfloat16),
        ),
        in_specs=[pl.BlockSpec(memory_space=pltpu.SMEM), pl.BlockSpec(memory_space=pltpu.VMEM)]
        + [anywhere] * len(pieces),
        out_specs=[pl.BlockSpec(memory_space=pltpu.VMEM)] * 2,
        scratch_shapes=[
            pltpu.VMEM((Z * YH, bs, width), jnp.bfloat16),
            pltpu.VMEM((blocks_out * CORE, bs, width), jnp.float32),
            pltpu.SemaphoreType.DMA((len(pieces),)),
        ],
        compiler_params=pltpu.CompilerParams(vmem_limit_bytes=32 * 2**20),
        cost_estimate=pl.CostEstimate(
            flops=2 * slots * bs * bs * width, bytes_accessed=8 * 2**20, transcendentals=0
        ),
    )(meta, values, *pieces)


def combine_kernel(keep, came, out):
    out[...] = (keep[...] + came[...].astype(jnp.float32)).astype(out.dtype)


def combine(keep, came):
    whole = pl.BlockSpec(memory_space=pltpu.VMEM)
    return pl.pallas_call(
        combine_kernel,
        out_shape=jax.ShapeDtypeStruct(keep.shape, jnp.bfloat16),
        in_specs=[whole, whole],
        out_specs=whole,
        compiler_params=pltpu.CompilerParams(vmem_limit_bytes=16 * 2**20),
        cost_estimate=pl.CostEstimate(flops=keep.size, bytes_accessed=8 * keep.size, transcendentals=0),
    )(keep, came)


def finish_kernel(pre, *refs):
    out = refs[-1]
    width = pre.shape[1] // PARTS
    for part in range(PARTS):
        terms = refs[part]
        total = terms[0].astype(jnp.float32)
        for k in range(1, YL * X):
            total = total + terms[k].astype(jnp.float32)
        cols = slice(part * width, (part + 1) * width)
        gate = pre[:, cols].astype(jnp.float32) > 0
        out[:, cols] = jnp.where(gate, total, 0.0).astype(out.dtype)


def finish(pre, terms):
    whole = pl.BlockSpec(memory_space=pltpu.VMEM)
    return pl.pallas_call(
        finish_kernel,
        out_shape=jax.ShapeDtypeStruct(pre.shape, jnp.bfloat16),
        in_specs=[whole] * (1 + len(terms)),
        out_specs=whole,
        compiler_params=pltpu.CompilerParams(vmem_limit_bytes=16 * 2**20),
        cost_estimate=pl.CostEstimate(flops=9 * pre.size, bytes_accessed=20 * pre.size, transcendentals=0),
    )(pre, *terms)


def gather_column(part):
    return [part, send(part, along_y(1)), send(part, along_y(2)), send(part, along_y(-1))]


def gather_rings(mine):
    low, high = [mine], [mine]
    for _ in range(Z // 2 - 1):
        low.append(send(low[-1], along_z(1)))
        high.append(send(high[-1], along_z(-1)))
    cut = YH // 2
    middle = [send(low[-1][:cut], along_z(1)), send(high[-1][cut:], along_z(-1))]
    return low + middle + high[:0:-1]


def reduce_part(keep, away):
    both = combine(keep, send(away, other_core))
    groups = [[CORE * k + core for k in range(YL * X)] for core in range(CORE)]
    return lax.all_to_all(both, "row", 0, 0, axis_index_groups=groups, tiled=True)


def shards(panel, blocks, block_rows, block_cols, block_count, pre_act):
    values = blocks[0, 0]
    col = lax.axis_index("col")
    core = (lax.axis_index("row") & 1).astype(jnp.int32)
    z, yh = col >> 2, col & (YH - 1)
    rows = block_rows[0, 0]
    near = ((z - (rows >> 2)) & (Z - 1)) * YH + ((yh - rows) & (YH - 1))
    meta = jnp.concatenate([near, block_cols[0, 0], block_count[0], core[None]])

    width = panel.shape[3] // PARTS
    column = gather_column(panel[0, 0])
    pieces = gather_rings(jnp.stack(column))
    values = fetch(meta, values)
    parts = [spmm(meta, values, pieces, p * width, width) for p in range(PARTS)]
    terms = [reduce_part(*part) for part in parts]
    return finish(pre_act[0, 0], terms)[None, None]


def solution(mesh):
    placed = (
        P("row", "col", None, None),
        P("row", "col", None, None, None),
        P("row", "col", None),
        P("row", "col", None),
        P("row", "col"),
        P("col", "row", None, None),
    )
    return jax.shard_map(
        shards, mesh=mesh, in_specs=placed, out_specs=P("col", "row", None, None), check_vma=False
    )
```
